32 devices in a mesh: ctx: 16 (over z, x, core), head: 2 (over y).
Axes of the slice: x: 2, y: 2, z: 4, core: 2. Of those that a mesh axis runs over, the one named last changes fastest.
Arguments:
- block_order: int32 [32], replicated, may hold values from 0 to 31, as said below
- queries: bfloat16 [6144, 4096], P('ctx', 'head'), may hold values from -12 to 12
- key_head_matrix: bfloat16 [6144, 1024], P('ctx', 'head'), may hold values from -6 to 6
- value_head_matrix: bfloat16 [6144, 1024], P('ctx', 'head'), may hold values from -6 to 6
- out_weight: bfloat16 [4096, 4096], P('head'), may hold values from -0.125 to 0.125
- filter_taps: float32 [128, 4096], P(None, 'head'), may hold values from -0.5 to 0.5
- skip_gain: float32 [4096], P('head'), may hold values from 0.5 to 1.5
- gate_values: bfloat16 [6144, 4096], P('ctx', 'head'), may hold values from -4 to 4
Outputs:
- mixed_out: bfloat16 [6144, 4096], P('ctx', 'head')
The draws below stay inside these ranges and needn't reach their ends.
Inputs may be any that keep to these rules, and one draw needn't show every extreme that they name: A permutation of the 32 sequence blocks; for every d, block_order[2 d] < 16 and block_order[2 d] + block_order[2 d + 1] = 31.
All inputs are finite; a program needn't handle non-finite values.
Results may differ from the reference program's by a relative error of at most 0.015.
Values may be sent and summed in bfloat16 or wider, within the bound.
A program may use at most 128 MiB of HBM per device.

```python
import math
import jax
import jax.numpy as jnp
from jax import lax

D = 4096
QUERY_HEADS = 32
KEY_VALUE_HEADS = 8
HEAD_WIDTH = 128
TAPS = 128
QUERY_PER_KV = 4
BLK = 192
NBLK = 32
SEQUENCE_ROWS = 6144
N_HEAD = 2


def draw_block_order(key, part):
    shuffled = jax.random.permutation(key, NBLK // 2).astype(jnp.int32)
    pair_order = jnp.stack([shuffled, NBLK - 1 - shuffled], axis=1)
    return pair_order.reshape(NBLK).astype(jnp.int32)


def query_key_pair(key):
    query_seed = jax.random.fold_in(key, 101)
    key_random_seed = jax.random.fold_in(key, 102)
    query_vals = jnp.clip(3.0 * jax.random.normal(query_seed, (SEQUENCE_ROWS, QUERY_HEADS * HEAD_WIDTH), jnp.float32), -12.0, 12.0)
    key_entries = jnp.clip(jax.random.normal(key_random_seed, (SEQUENCE_ROWS, KEY_VALUE_HEADS * HEAD_WIDTH), jnp.float32), -6.0, 6.0)
    return (query_vals, key_entries)


def draw_queries(key, part):
    return query_key_pair(key)[0].astype(jnp.bfloat16)


def draw_key_head_matrix(key, part):
    return query_key_pair(key)[1].astype(jnp.bfloat16)


def raised(array, stream_key, source, target, blocks, factor):
    def block_of(position):
        return (jnp.arange(array.shape[position]) // (array.shape[position] // blocks)).reshape((-1,) + (1,) * (array.ndim - 1 - position))

    first = jax.random.permutation(stream_key, blocks)[block_of(target)]
    other_side = (block_of(target) + blocks // 2) % blocks
    return jnp.where((block_of(source) == first) | (block_of(source) == other_side), factor * array, array)


def shard_levels(rng, extent, split, least, largest):
    factor_of, own = 1.0, jax.random.fold_in(rng, 6)
    for axis_at, blocks in split:
        draws = jnp.exp(jax.random.uniform(jax.random.fold_in(own, axis_at), (blocks,), jnp.float32, least / len(split), largest / len(split)))
        factor_of = factor_of * jnp.repeat(draws, extent[axis_at] // blocks).reshape([-1 if axis == axis_at else 1 for axis in range(len(extent))])
    return factor_of


def bell_draw(own_key, shape, spread, bound, cuts=(), held_as=jnp.bfloat16):
    values = spread * jax.random.normal(own_key, shape, jnp.float32)
    if cuts:
        values = values * shard_levels(own_key, shape, cuts, -0.22, 0.18)
    return jnp.clip(values, -bound, bound).astype(held_as)


def gaussian_with(key, shape, deviation, bound, shards, heavy, held_as=jnp.bfloat16):
    values = deviation * jax.random.normal(key, shape, jnp.float32)
    if shards:
        values = values * shard_levels(key, shape, shards, -0.22, 0.18)
    return jnp.clip(raised(values, jax.random.fold_in(key, 3), *heavy), -bound, bound).astype(held_as)


def setup_inputs(seed: int = 0) -> dict:
    arg_keys = jax.random.split(jax.random.key(seed), 9)
    block_order = draw_block_order(jax.random.fold_in(arg_keys[8], 71), 0)
    queries = draw_queries(jax.random.fold_in(arg_keys[8], 71), 0)
    key_head_matrix = draw_key_head_matrix(jax.random.fold_in(arg_keys[8], 71), 0)
    value_head_matrix = bell_draw(arg_keys[3], (SEQUENCE_ROWS, KEY_VALUE_HEADS * HEAD_WIDTH), 1.0, 6.0, ((0, 16), (1, 2)))
    out_weight = gaussian_with(arg_keys[4], (QUERY_HEADS * HEAD_WIDTH, D), (QUERY_HEADS * HEAD_WIDTH) ** -0.5, 0.125, ((0, 2),), (0, 1, 2, 2.0))
    filter_taps = bell_draw(arg_keys[5], (TAPS, D), TAPS ** -0.5, 0.5, ((1, 2),), jnp.float32)
    skip_gain = jnp.clip(0.5 + 1.0 * jax.random.uniform(arg_keys[6], (D,), jnp.float32) ** shard_levels(arg_keys[6], (D,), ((0, 2),), -0.2, 0.2), 0.5, 1.5)
    gate_values = bell_draw(arg_keys[7], (SEQUENCE_ROWS, D), 1.0, 4.0, ((0, 16), (1, 2)))
    return {"block_order": block_order, "queries": queries, "key_head_matrix": key_head_matrix, "value_head_matrix": value_head_matrix, "out_weight": out_weight, "filter_taps": filter_taps, "skip_gain": skip_gain, "gate_values": gate_values}


def inverse_order(block_order):
    return jnp.zeros((NBLK,), jnp.int32).at[block_order].set(jnp.arange(NBLK, dtype=jnp.int32))

def reference(block_order, queries, key_head_matrix, value_head_matrix, out_weight, filter_taps, skip_gain, gate_values):
    holder = inverse_order(block_order)

    def restore_sequence_order(array_in):
        return array_in.reshape(NBLK, BLK, -1)[holder].reshape(SEQUENCE_ROWS, -1)

    def to_layout(array_in):
        return array_in.reshape(NBLK, BLK, -1)[block_order].reshape(SEQUENCE_ROWS, -1)
    query_sequence = restore_sequence_order(queries).reshape(SEQUENCE_ROWS, KEY_VALUE_HEADS, QUERY_PER_KV, HEAD_WIDTH)
    key_sequence = restore_sequence_order(key_head_matrix).reshape(SEQUENCE_ROWS, KEY_VALUE_HEADS, HEAD_WIDTH)
    value_sequence = restore_sequence_order(value_head_matrix).reshape(SEQUENCE_ROWS, KEY_VALUE_HEADS, HEAD_WIDTH)
    width = math.gcd(SEQUENCE_ROWS, 512)
    scaling = 1.0 / math.sqrt(HEAD_WIDTH)
    outputs = []
    for number in range(SEQUENCE_ROWS // width):
        finish = (number + 1) * width
        query_part = jnp.moveaxis(query_sequence[number * width:finish], 1, 0)
        key_part = jnp.moveaxis(key_sequence[:finish], 1, 0)
        value_part = jnp.moveaxis(value_sequence[:finish], 1, 0)
        query_place = number * width + jnp.arange(width, dtype=jnp.int32)
        key_place = jnp.arange(finish, dtype=jnp.int32)
        allowed = key_place[None, :] <= query_place[:, None]

        def one_group(operands):
            group_query, group_key, group_value = operands
            scores = jnp.einsum('qgd,kd->gqk', group_query.astype(jnp.float32), group_key.astype(jnp.float32)) * scaling
            scores = jnp.where(allowed[None], scores, -jnp.inf)
            row_max = lax.optimization_barrier(jnp.max(scores, axis=-1, keepdims=True))
            weight = jnp.where(allowed[None], jnp.exp(scores - row_max), 0.0)
            row_total = lax.optimization_barrier(jnp.sum(weight, axis=-1))
            rounded = lax.optimization_barrier(weight.astype(jnp.bfloat16)).astype(jnp.float32)
            summed = jnp.einsum('gqk,kd->qgd', rounded, group_value.astype(jnp.float32))
            return summed / jnp.transpose(row_total)[:, :, None]
        attended = lax.map(one_group, (query_part, key_part, value_part))
        outputs.append(jnp.moveaxis(attended, 0, 1).reshape(width, QUERY_HEADS * HEAD_WIDTH))
    attended = jnp.concatenate(outputs, axis=0).astype(jnp.bfloat16)
    share_cols = QUERY_HEADS * HEAD_WIDTH // N_HEAD
    projected = jnp.zeros((SEQUENCE_ROWS, D), jnp.float32)
    for group in range(N_HEAD):
        partial_value = jnp.dot(attended[:, group * share_cols:(group + 1) * share_cols], out_weight[group * share_cols:(group + 1) * share_cols], preferred_element_type=jnp.float32)
        projected = projected + lax.optimization_barrier(partial_value.astype(jnp.bfloat16)).astype(jnp.float32)
    projected = projected.astype(jnp.bfloat16)
    source = projected.astype(jnp.float32)
    padded = jnp.concatenate([jnp.zeros((TAPS - 1, D), jnp.float32), source], axis=0)

    def add_tap(tap_index, running):
        begin = (TAPS - 1 - tap_index).astype(jnp.int32)
        return running + filter_taps[tap_index][None, :] * lax.dynamic_slice_in_dim(padded, begin, SEQUENCE_ROWS, 0)
    filtered = lax.fori_loop(0, TAPS, add_tap, jnp.zeros((SEQUENCE_ROWS, D), jnp.float32))
    gate_seq = restore_sequence_order(gate_values).astype(jnp.float32)
    mixed_rows = gate_seq * (filtered + skip_gain[None, :] * source)
    return to_layout(mixed_rows.astype(jnp.bfloat16))
```

```python
import functools
import math

import jax
import jax.numpy as jnp
import ml_dtypes
import numpy as np
from jax import lax
from jax.experimental import pallas as pl
from jax.experimental.pallas import tpu as pltpu
from jax.sharding import PartitionSpec as P

HEAD_WIDTH = 128
QUERY_PER_KV = 4
VMEM_LIMIT = 56 * 1024 * 1024


def attention_kernel(order_ref, holder_ref, q_ref, k_ref, v_ref, out_ref, *, block_rows, devices, chunk):
    factor = math.log2(math.e) / math.sqrt(HEAD_WIDTH)
    rows = QUERY_PER_KV * block_rows

    def update(state, q, k, v, mask=None):
        top, acc = state
        s = lax.dot_general(q, k, (((1,), (1,)), ((), ())), preferred_element_type=jnp.float32) * factor
        if mask is not None:
            s = jnp.where(mask, s, -1e30)
        new_top = jnp.maximum(top, jnp.max(s, axis=1, keepdims=True))
        p = jnp.exp2(s - new_top)
        fade = jnp.exp2(top - new_top)
        v_ext = jnp.concatenate([v, jnp.ones_like(v)], axis=1)
        acc = acc * fade + jnp.dot(p.astype(jnp.bfloat16), v_ext, preferred_element_type=jnp.float32)
        return new_top, acc

    row_at = lax.broadcasted_iota(jnp.int32, (rows, block_rows), 0)
    row_at = lax.rem(row_at, block_rows)
    col_at = lax.broadcasted_iota(jnp.int32, (rows, block_rows), 1)
    diagonal = col_at <= row_at

    for half in range(2):
        q = jnp.concatenate(
            [
                q_ref[pl.ds(half * block_rows, block_rows), pl.ds(g * HEAD_WIDTH, HEAD_WIDTH)]
                for g in range(QUERY_PER_KV)
            ],
            axis=0,
        )
        own = holder_ref[order_ref[half]] // 2
        state = (
            jnp.full((rows, 1), -1e30, jnp.float32),
            jnp.zeros((rows, 2 * HEAD_WIDTH), jnp.float32),
        )
        state = update(state, q, k_ref[own, half], v_ref[own, half], diagonal)
        if half == 1:

            def low_step(i, state):
                k = k_ref[pl.ds(i * chunk, chunk), 0].reshape(chunk * block_rows, HEAD_WIDTH)
                v = v_ref[pl.ds(i * chunk, chunk), 0].reshape(chunk * block_rows, HEAD_WIDTH)
                return update(state, q, k, v)

            state = lax.fori_loop(0, devices // chunk, low_step, state)

        def step(j, state):
            at = holder_ref[j] // 2
            return update(state, q, k_ref[at, half], v_ref[at, half])

        state = lax.fori_loop(half * devices, order_ref[half], step, state)
        acc = state[1]
        result = (acc[:, :HEAD_WIDTH] / acc[:, HEAD_WIDTH:]).astype(jnp.bfloat16)
        for g in range(QUERY_PER_KV):
            out_ref[pl.ds(half * block_rows, block_rows), pl.ds(g * HEAD_WIDTH, HEAD_WIDTH)] = result[
                g * block_rows : (g + 1) * block_rows
            ]


def attention(own_order, holder, queries, keys, values, block_rows):
    local_rows, width = queries.shape
    devices = keys.shape[0]
    kv_heads = keys.shape[3] // HEAD_WIDTH
    group = QUERY_PER_KV * HEAD_WIDTH
    kv_spec = pl.BlockSpec((devices, 2, block_rows, HEAD_WIDTH), lambda h, *_: (0, 0, 0, h))
    return pl.pallas_call(
        functools.partial(
            attention_kernel, block_rows=block_rows, devices=devices, chunk=math.gcd(devices, 4)
        ),
        grid_spec=pltpu.PrefetchScalarGridSpec(
            num_scalar_prefetch=2,
            grid=(kv_heads,),
            in_specs=[pl.BlockSpec((local_rows, group), lambda h, *_: (0, h)), kv_spec, kv_spec],
            out_specs=pl.BlockSpec((local_rows, group), lambda h, *_: (0, h)),
        ),
        out_shape=jax.ShapeDtypeStruct((local_rows, width), jnp.bfloat16),
        compiler_params=pltpu.CompilerParams(vmem_limit_bytes=VMEM_LIMIT),
        name="attention",
    )(own_order, holder, queries, keys, values)


def split_bf16(array):
    high = array.astype(ml_dtypes.bfloat16)
    low = (array - high.astype(np.float64)).astype(ml_dtypes.bfloat16)
    return high, low


def transform_tables(taps, block_rows):
    size = taps + block_rows
    freq = np.arange(size // 2)[:, None] + 0.5
    angle = 2.0 * np.pi * freq * np.arange(size)[None, :] / size
    forward = np.concatenate([np.cos(angle), -np.sin(angle)], axis=0)
    back = np.concatenate([np.cos(angle), -np.sin(angle)], axis=0).T * (2.0 / size)
    back = back[taps:]
    fh, fl = split_bf16(forward)
    bh, bl = split_bf16(back)
    tap_table = np.concatenate([fh[:, :taps], fh[:, :taps], fl[:, :taps]], axis=1)
    signal_table = np.concatenate([fh, fl], axis=0)
    back_table = np.concatenate([bh, bh, bl], axis=1)
    return jnp.asarray(tap_table), jnp.asarray(signal_table), jnp.asarray(back_table)


def three_parts(x):
    high = x.astype(jnp.bfloat16)
    low = (x - high.astype(jnp.float32)).astype(jnp.bfloat16)
    return jnp.concatenate([high, low, high], axis=0)


def filter_kernel(tap_table, signal_table, back_table, taps_ref, skip_ref, halo_ref, x_ref, gate_ref, out_ref, *, block_rows):
    size = signal_table.shape[1]
    half_size = size // 2
    spectrum = jnp.dot(tap_table[...], three_parts(taps_ref[...]), preferred_element_type=jnp.float32)
    h_re, h_im = spectrum[:half_size], spectrum[half_size:]
    for block in range(2):
        rows = pl.ds(block * block_rows, block_rows)
        here = x_ref[rows, :]
        signal = jnp.concatenate([halo_ref[block], here], axis=0)
        both = jnp.dot(signal_table[...], signal, preferred_element_type=jnp.float32)
        both = both[:size] + both[size:]
        re, im = both[:half_size], both[half_size:]
        product = jnp.concatenate([re * h_re - im * h_im, re * h_im + im * h_re], axis=0)
        filtered = jnp.dot(back_table[...], three_parts(product), preferred_element_type=jnp.float32)
        mixed = gate_ref[rows, :].astype(jnp.float32) * (filtered + skip_ref[...] * here.astype(jnp.float32))
        out_ref[rows, :] = mixed.astype(jnp.bfloat16)


def causal_filter(projected, halo, filter_taps, skip_gain, gate_values, block_rows):
    local_rows, channels = projected.shape
    taps = filter_taps.shape[0]
    tables = transform_tables(taps, block_rows)
    tile = math.gcd(channels, 256)
    whole = [pl.BlockSpec(t.shape, lambda c: (0, 0)) for t in tables]
    rows_spec = pl.BlockSpec((local_rows, tile), lambda c: (0, c))
    return pl.pallas_call(
        functools.partial(filter_kernel, block_rows=block_rows),
        grid=(channels // tile,),
        in_specs=whole
        + [
            pl.BlockSpec((taps, tile), lambda c: (0, c)),
            pl.BlockSpec((1, tile), lambda c: (0, c)),
            pl.BlockSpec((2, taps, tile), lambda c: (0, 0, c)),
            rows_spec,
            rows_spec,
        ],
        out_specs=rows_spec,
        out_shape=jax.ShapeDtypeStruct((local_rows, channels), jnp.bfloat16),
        compiler_params=pltpu.CompilerParams(vmem_limit_bytes=VMEM_LIMIT),
        name="causal_filter",
    )(*tables, filter_taps, skip_gain[None, :], halo, projected, gate_values)


def shards(
    block_order,
    queries,
    key_head_matrix,
    value_head_matrix,
    out_weight,
    filter_taps,
    skip_gain,
    gate_values,
):
    local_rows = queries.shape[0]
    block_rows = local_rows // 2
    kv_width = key_head_matrix.shape[1]
    taps = filter_taps.shape[0]
    blocks = block_order.shape[0]
    devices = blocks // 2
    position = lax.axis_index("ctx")
    numbers = jnp.arange(blocks, dtype=jnp.int32)
    at_block = block_order[None, :] == numbers[:, None]
    holder = jnp.sum(jnp.where(at_block, numbers[None, :], 0), axis=1)
    own_order = lax.dynamic_slice(block_order, (2 * position,), (2,))

    keys = lax.all_gather(key_head_matrix, "ctx", axis=0, tiled=True)
    values = lax.all_gather(value_head_matrix, "ctx", axis=0, tiled=True)
    keys = keys.reshape(devices, 2, block_rows, kv_width)
    values = values.reshape(devices, 2, block_rows, kv_width)
    attended = attention(own_order, holder, queries, keys, values, block_rows)
    partials = jnp.dot(attended, out_weight, preferred_element_type=jnp.float32)
    projected = lax.psum_scatter(
        partials.astype(jnp.bfloat16), "head", scatter_dimension=1, tiled=True
    )
    channels = projected.shape[1]
    tails = projected.reshape(2, block_rows, channels)[:, block_rows - taps :, :]
    slices = lax.all_to_all(tails, "ctx", split_axis=1, concat_axis=0, tiled=True)
    wanted = (block_order[None, :] == block_order[:, None] - 1).astype(jnp.bfloat16)
    routed = jnp.dot(
        wanted, slices.reshape(blocks, -1), preferred_element_type=jnp.float32
    ).astype(jnp.bfloat16)
    routed = routed.reshape(slices.shape)
    halo = lax.all_to_all(routed, "ctx", split_axis=0, concat_axis=1, tiled=True)
    return causal_filter(projected, halo, filter_taps, skip_gain, gate_values, block_rows)


def solution(mesh):
    return jax.shard_map(
        shards,
        mesh=mesh,
        in_specs=(
            P(),
            P("ctx", "head"),
            P("ctx", "head"),
            P("ctx", "head"),
            P("head", None),
            P(None, "head"),
            P("head"),
            P("ctx", "head"),
        ),
        out_specs=P("ctx", "head"),
        check_vma=False,
    )
```

```python
import functools
import math

import jax
import jax.numpy as jnp
import ml_dtypes
import numpy as np
from jax import lax
from jax.experimental import pallas as pl
from jax.experimental.pallas import tpu as pltpu
from jax.sharding import PartitionSpec as P

HEAD_WIDTH = 128
QUERY_PER_KV = 4
VMEM_LIMIT = 56 * 1024 * 1024


def attention_kernel(order_ref, holder_ref, q_ref, k_ref, v_ref, out_ref, *, block_rows, devices, chunk):
    factor = math.log2(math.e) / math.sqrt(HEAD_WIDTH)
    rows = QUERY_PER_KV * block_rows

    def update(state, q, k, v, mask=None):
        top, acc = state
        s = lax.dot_general(q, k, (((1,), (1,)), ((), ())), preferred_element_type=jnp.float32) * factor
        if mask is not None:
            s = jnp.where(mask, s, -1e30)
        new_top = jnp.maximum(top, jnp.max(s, axis=1, keepdims=True))
        p = jnp.exp2(s - new_top)
        fade = jnp.exp2(top - new_top)
        v_ext = jnp.concatenate([v, jnp.ones_like(v)], axis=1)
        acc = acc * fade + jnp.dot(p.astype(jnp.bfloat16), v_ext, preferred_element_type=jnp.float32)
        return new_top, acc

    row_at = lax.broadcasted_iota(jnp.int32, (rows, block_rows), 0)
    row_at = lax.rem(row_at, block_rows)
    col_at = lax.broadcasted_iota(jnp.int32, (rows, block_rows), 1)
    diagonal = col_at <= row_at

    for half in range(2):
        q = jnp.concatenate(
            [
                q_ref[pl.ds(half * block_rows, block_rows), pl.ds(g * HEAD_WIDTH, HEAD_WIDTH)]
                for g in range(QUERY_PER_KV)
            ],
            axis=0,
        )
        own = holder_ref[order_ref[half]] // 2
        state = (
            jnp.full((rows, 1), -1e30, jnp.float32),
            jnp.zeros((rows, 2 * HEAD_WIDTH), jnp.float32),
        )
        state = update(state, q, k_ref[own, half], v_ref[own, half], diagonal)
        if half == 1:

            def low_step(i, state):
                k = k_ref[pl.ds(i * chunk, chunk), 0].reshape(chunk * block_rows, HEAD_WIDTH)
                v = v_ref[pl.ds(i * chunk, chunk), 0].reshape(chunk * block_rows, HEAD_WIDTH)
                return update(state, q, k, v)

            state = lax.fori_loop(0, devices // chunk, low_step, state)

        def step(j, state):
            at = holder_ref[j] // 2
            return update(state, q, k_ref[at, half], v_ref[at, half])

        state = lax.fori_loop(half * devices, order_ref[half], step, state)
        acc = state[1]
        result = (acc[:, :HEAD_WIDTH] / acc[:, HEAD_WIDTH:]).astype(jnp.bfloat16)
        for g in range(QUERY_PER_KV):
            out_ref[pl.ds(half * block_rows, block_rows), pl.ds(g * HEAD_WIDTH, HEAD_WIDTH)] = result[
                g * block_rows : (g + 1) * block_rows
            ]


def attention(own_order, holder, queries, pairs, head, block_rows):
    local_rows = queries.shape[0]
    devices = pairs.shape[0]
    group = QUERY_PER_KV * HEAD_WIDTH
    pair_block = (devices, 2, block_rows, HEAD_WIDTH)
    work = 2 * QUERY_PER_KV * block_rows * (devices + 1) * 2 * block_rows
    return pl.pallas_call(
        functools.partial(
            attention_kernel, block_rows=block_rows, devices=devices, chunk=math.gcd(devices, 4)
        ),
        grid_spec=pltpu.PrefetchScalarGridSpec(
            num_scalar_prefetch=2,
            grid=(1,),
            in_specs=[
                pl.BlockSpec((local_rows, group), lambda i, *_: (0, head)),
                pl.BlockSpec(pair_block, lambda i, *_: (0, 0, 0, 0)),
                pl.BlockSpec(pair_block, lambda i, *_: (0, 0, 0, 1)),
            ],
            out_specs=pl.BlockSpec((local_rows, group), lambda i, *_: (0, 0)),
        ),
        out_shape=jax.ShapeDtypeStruct((local_rows, group), jnp.bfloat16),
        compiler_params=pltpu.CompilerParams(vmem_limit_bytes=VMEM_LIMIT),
        cost_estimate=pl.CostEstimate(
            flops=work * 4 * HEAD_WIDTH, bytes_accessed=2 * pairs.size, transcendentals=work
        ),
        name="attention",
    )(own_order, holder, queries, pairs, pairs)


def split_bf16(array):
    high = array.astype(ml_dtypes.bfloat16)
    low = (array - high.astype(np.float64)).astype(ml_dtypes.bfloat16)
    return high, low


def transform_tables(taps, block_rows):
    size = taps + block_rows
    freq = np.arange(size // 2)[:, None] + 0.5
    angle = 2.0 * np.pi * freq * np.arange(size)[None, :] / size
    forward = np.concatenate([np.cos(angle), -np.sin(angle)], axis=0)
    back = np.concatenate([np.cos(angle), -np.sin(angle)], axis=0).T * (2.0 / size)
    back = back[taps:]
    fh, fl = split_bf16(forward)
    bh, bl = split_bf16(back)
    tap_table = np.concatenate([fh[:, :taps], fh[:, :taps], fl[:, :taps]], axis=1)
    signal_table = np.concatenate([fh, fl], axis=0)
    back_table = np.concatenate([bh, bh, bl], axis=1)
    return jnp.asarray(tap_table), jnp.asarray(signal_table), jnp.asarray(back_table)


def three_parts(x):
    high = x.astype(jnp.bfloat16)
    low = (x - high.astype(jnp.float32)).astype(jnp.bfloat16)
    return jnp.concatenate([high, low, high], axis=0)


def filter_kernel(tap_table, signal_table, back_table, taps_ref, skip_ref, halo_ref, x_ref, gate_ref, out_ref, *, block_rows):
    size = signal_table.shape[1]
    half_size = size // 2
    spectrum = jnp.dot(tap_table[...], three_parts(taps_ref[...]), preferred_element_type=jnp.float32)
    h_re, h_im = spectrum[:half_size], spectrum[half_size:]
    for block in range(2):
        rows = pl.ds(block * block_rows, block_rows)
        here = x_ref[rows, :]
        signal = jnp.concatenate([halo_ref[block], here], axis=0)
        both = jnp.dot(signal_table[...], signal, preferred_element_type=jnp.float32)
        both = both[:size] + both[size:]
        re, im = both[:half_size], both[half_size:]
        product = jnp.concatenate([re * h_re - im * h_im, re * h_im + im * h_re], axis=0)
        filtered = jnp.dot(back_table[...], three_parts(product), preferred_element_type=jnp.float32)
        mixed = gate_ref[rows, :].astype(jnp.float32) * (filtered + skip_ref[...] * here.astype(jnp.float32))
        out_ref[rows, :] = mixed.astype(jnp.bfloat16)


def causal_filter(projected, halo, filter_taps, skip_gain, gate_values, block_rows):
    local_rows, channels = projected.shape
    taps = filter_taps.shape[0]
    tables = transform_tables(taps, block_rows)
    tile = math.gcd(channels, 256)
    whole = [pl.BlockSpec(t.shape, lambda c: (0, 0)) for t in tables]
    rows_spec = pl.BlockSpec((local_rows, tile), lambda c: (0, c))
    return pl.pallas_call(
        functools.partial(filter_kernel, block_rows=block_rows),
        grid=(channels // tile,),
        in_specs=whole
        + [
            pl.BlockSpec((taps, tile), lambda c: (0, c)),
            pl.BlockSpec((1, tile), lambda c: (0, c)),
            pl.BlockSpec((2, taps, tile), lambda c: (0, 0, c)),
            rows_spec,
            rows_spec,
        ],
        out_specs=rows_spec,
        out_shape=jax.ShapeDtypeStruct((local_rows, channels), jnp.bfloat16),
        compiler_params=pltpu.CompilerParams(vmem_limit_bytes=VMEM_LIMIT),
        name="causal_filter",
    )(*tables, filter_taps, skip_gain[None, :], halo, projected, gate_values)


def shards(
    block_order,
    queries,
    key_head_matrix,
    value_head_matrix,
    out_weight,
    filter_taps,
    skip_gain,
    gate_values,
):
    local_rows = queries.shape[0]
    block_rows = local_rows // 2
    kv_width = key_head_matrix.shape[1]
    taps = filter_taps.shape[0]
    blocks = block_order.shape[0]
    devices = blocks // 2
    position = lax.axis_index("ctx")
    numbers = jnp.arange(blocks, dtype=jnp.int32)
    at_block = block_order[None, :] == numbers[:, None]
    holder = jnp.sum(jnp.where(at_block, numbers[None, :], 0), axis=1)
    own_order = lax.dynamic_slice(block_order, (2 * position,), (2,))

    gathered = []
    for head in range(kv_width // HEAD_WIDTH):
        columns = slice(head * HEAD_WIDTH, (head + 1) * HEAD_WIDTH)
        pair = jnp.concatenate([key_head_matrix[:, columns], value_head_matrix[:, columns]], axis=1)
        pairs = lax.all_gather(pair, "ctx", axis=0, tiled=True)
        gathered.append(pairs.reshape(devices, 2, block_rows, 2 * HEAD_WIDTH))
    attended = jnp.concatenate(
        [
            attention(own_order, holder, queries, pairs, head, block_rows)
            for head, pairs in enumerate(gathered)
        ],
        axis=1,
    )
    partials = jnp.dot(attended, out_weight, preferred_element_type=jnp.float32)
    projected = lax.psum_scatter(
        partials.astype(jnp.bfloat16), "head", scatter_dimension=1, tiled=True
    )
    channels = projected.shape[1]
    tails = projected.reshape(2, block_rows, channels)[:, block_rows - taps :, :]
    slices = lax.all_to_all(tails, "ctx", split_axis=1, concat_axis=0, tiled=True)
    wanted = (block_order[None, :] == block_order[:, None] - 1).astype(jnp.bfloat16)
    routed = jnp.dot(
        wanted, slices.reshape(blocks, -1), preferred_element_type=jnp.float32
    ).astype(jnp.bfloat16)
    routed = routed.reshape(slices.shape)
    halo = lax.all_to_all(routed, "ctx", split_axis=0, concat_axis=1, tiled=True)
    return causal_filter(projected, halo, filter_taps, skip_gain, gate_values, block_rows)


def solution(mesh):
    return jax.shard_map(
        shards,
        mesh=mesh,
        in_specs=(
            P(),
            P("ctx", "head"),
            P("ctx", "head"),
            P("ctx", "head"),
            P("head", None),
            P(None, "head"),
            P("head"),
            P("ctx", "head"),
        ),
        out_specs=P("ctx", "head"),
        check_vma=False,
    )
```
